1024 devices in a mesh: dp: 32 (over x, z_hi, core), mx: 4 (over y), my: 8 (over z_lo).
Axes of the slice: x: 4, y: 4, z: 32 (z_hi: 4, z_lo: 8; z = z_hi * 8 + z_lo), core: 2. Of those that a mesh axis runs over, the one named last changes fastest.
Arguments:
- saved_block_input: bfloat16 [8192, 6144], P('dp', 'mx'), may hold values from -6 to 6
- token_row_mean: float32 [8192], P('dp'), may hold values from -3 to 3
- qk_weight: bfloat16 [6144, 2, 3072], P('mx', None, 'my'), may hold values from -0.078125 to 0.078125
- norm_grads: bfloat16 [8192, 2, 3072], P('dp', None, 'my'), may hold values from -6 to 6
Outputs:
- block_input_gradient: bfloat16 [8192, 6144], P(('dp', 'my'), 'mx')
- weight_grad: float32 [6144, 2, 3072], P(('mx', 'dp'), None, 'my')
The draws below stay inside these ranges and needn't reach their ends.
All inputs are finite; a program needn't handle non-finite values.
Results may differ from the reference program's by a relative error of at most 0.02.
Values may be sent and summed in bfloat16 or wider, within the bound.
No kernel may reach another device: no remote copies, remote signals or barrier semaphores. Data moves between devices by JAX's collectives and lax.ppermute only.
A program may use at most 32 MiB of HBM per device.

```python
import jax
import jax.numpy as jnp
from jax import lax

D = 6144
HEAD_DIM = 128
TOK = 256
HD = 3072
TOKENS = 8192
N_DP = 32
N_MX = 4
N_MY = 8


def spiked(values, key, source, target, parts, factor):
    owner, partner = [(jnp.arange(values.shape[position]) // (values.shape[position] // parts)).reshape([-1 if axis == position else 1 for axis in range(values.ndim)]) for position in (source, target)]
    chosen = jax.random.permutation(key, parts)[partner]
    strong = (owner == chosen) | (owner == (partner + parts // 2) % parts)
    return jnp.where(strong, factor * values, values)


def block_scale(rng, shape, cuts, smallest, high):
    loudness = 1.0
    for position, parts in cuts:
        steps = jax.random.uniform(jax.random.fold_in(jax.random.fold_in(rng, 6), position), (parts,), jnp.float32, smallest / len(cuts), high / len(cuts))
        loudness = loudness * jnp.repeat(jnp.exp(steps), shape[position] // parts).reshape((-1,) + (1,) * (len(shape) - 1 - position))
    return loudness


def scatter_about(own_key, dims, scale, reach, cuts=(), dtype=jnp.bfloat16):
    values = jax.random.normal(own_key, dims, jnp.float32) * scale
    if len(cuts) > 0:
        values = block_scale(own_key, dims, cuts, -0.22, 0.18) * values
    return jnp.clip(values, min=-reach, max=reach).astype(dtype)


def gaussian_with(rng, dims, deviation, reach, shards, heavy, kind=jnp.bfloat16):
    drawn = deviation * jax.random.normal(rng, dims, jnp.float32)
    if shards:
        drawn = drawn * block_scale(rng, dims, shards, -0.22, 0.18)
    return jnp.clip(spiked(drawn, jax.random.fold_in(rng, 3), *heavy), -reach, reach).astype(kind)


def setup_inputs(seed: int = 0) -> dict:
    key_of = jax.random.split(jax.random.key(seed), 5)
    saved_block_input = gaussian_with(key_of[0], (TOKENS, D), 1.0, 6.0, ((0, 32), (1, 4)), (0, 1, 32, 2.75))
    token_row_mean = scatter_about(key_of[1], (TOKENS,), 0.5, 3.0, ((0, 32),), jnp.float32)
    qk_weight = scatter_about(key_of[2], (D, 2, HD), D ** -0.5, 0.078125, ((0, 4), (2, 8)))
    norm_grads = scatter_about(key_of[3], (TOKENS, 2, HD), 1.0, 6.0, ((0, 32), (2, 8)))
    return {"saved_block_input": saved_block_input, "token_row_mean": token_row_mean, "qk_weight": qk_weight, "norm_grads": norm_grads}


def head_norm_back(raw, grads):
    rows = raw.shape[0]
    shaped = raw.reshape(rows, 2, -1, HEAD_DIM)
    upstream = grads.astype(jnp.float32).reshape(rows, 2, -1, HEAD_DIM)
    centre = lax.optimization_barrier(jnp.mean(shaped, axis=-1, keepdims=True))
    spread = lax.rsqrt(lax.optimization_barrier(jnp.mean((shaped - centre) ** 2, axis=-1, keepdims=True)) + 1e-06)
    normal = (shaped - centre) * spread
    mean_grad = lax.optimization_barrier(jnp.mean(upstream, axis=-1, keepdims=True))
    mean_cross = lax.optimization_barrier(jnp.mean(upstream * normal, axis=-1, keepdims=True))
    d_raw = spread * (upstream - mean_grad - normal * mean_cross)
    return d_raw.reshape(rows, -1).astype(jnp.bfloat16)

def rounded(value):
    return lax.optimization_barrier(value.astype(jnp.bfloat16)).astype(jnp.float32)

def reference(saved_block_input, token_row_mean, qk_weight, norm_grads):
    centred_input = saved_block_input.astype(jnp.float32) - token_row_mean[:, None]
    normed_rows = centred_input.astype(jnp.bfloat16)
    flat_w = qk_weight.reshape(D, 2 * HD)
    feat = D // N_MX
    raw = jnp.zeros((TOKENS, 2 * HD), jnp.float32)
    for block in range(N_MX):
        part = jnp.dot(normed_rows[:, block * feat:(block + 1) * feat], flat_w[block * feat:(block + 1) * feat], preferred_element_type=jnp.float32)
        raw = raw + rounded(part)
    d_raw = head_norm_back(raw, norm_grads.reshape(TOKENS, 2 * HD))
    d_three = d_raw.reshape(TOKENS, 2, HD)
    cols = HD // N_MY
    normed_gradient = jnp.zeros((TOKENS, D), jnp.float32)
    for block in range(N_MY):
        left = d_three[:, :, block * cols:(block + 1) * cols].reshape(TOKENS, 2 * cols)
        right = qk_weight[:, :, block * cols:(block + 1) * cols].reshape(D, 2 * cols)
        part = lax.dot_general(left, right, (((1,), (1,)), ((), ())), preferred_element_type=jnp.float32)
        normed_gradient = normed_gradient + rounded(part)
    first_mean_term = lax.optimization_barrier(jnp.mean(normed_gradient, axis=1, keepdims=True))
    second_mean_term = lax.optimization_barrier(jnp.mean(normed_gradient * centred_input, axis=1, keepdims=True))
    block_input_gradient = (normed_gradient - first_mean_term - centred_input * second_mean_term).astype(jnp.bfloat16)
    group_normed = normed_rows.reshape(N_DP, TOK, D)
    group_draw = d_raw.reshape(N_DP, TOK, 2 * HD)

    def accumulate(total, pair):
        part = lax.dot_general(pair[0], pair[1], (((0,), (0,)), ((), ())), preferred_element_type=jnp.float32)
        return (total + rounded(part), None)
    total, unused = lax.scan(accumulate, jnp.zeros((D, 2 * HD), jnp.float32), (group_normed, group_draw))
    return (block_input_gradient, total.reshape(D, 2, HD))
```

```python
import functools

import jax
import jax.numpy as jnp
from jax import lax
from jax.experimental import pallas as pl
from jax.experimental.pallas import tpu as pltpu
from jax.sharding import Mesh, PartitionSpec as P

D = 6144
HEAD_DIM = 128
CHUNKS = (0, 4, 2, 6, 1, 5, 3, 7)
TOK = 256
CHUNK = 32
EXTRA = 16
BLOCK = 48


def chunk_rows(k):
    place = lax.axis_index("my")
    return pl.ds(pl.multiple_of(lax.bitwise_xor(place, k) * CHUNK, CHUNK), CHUNK)


def pairings(z, c):
    near, wrap = lax.bitwise_xor(z, 1), 3 - z
    first = jnp.where(c == 0, near, wrap)
    second = jnp.where(c == 0, wrap, near)
    return first, second


def project_kernel(x_ref, mean_ref, w_ref, send_ref, own_ref, other_ref, normed, turned):
    for place, k in enumerate(CHUNKS):
        rows = chunk_rows(k)
        centred = x_ref[rows, :].astype(jnp.float32) - mean_ref[rows, :]
        normed[place * CHUNK : (place + 1) * CHUNK, :] = centred.astype(jnp.bfloat16)
    w = w_ref[...]
    part = jnp.dot(normed[...], w, preferred_element_type=jnp.float32).astype(jnp.bfloat16)
    ones = jnp.ones((EXTRA, w.shape[0]), jnp.bfloat16)
    sums = jnp.dot(ones, w, preferred_element_type=jnp.float32)
    high = sums.astype(jnp.bfloat16).astype(jnp.float32)
    row = lax.broadcasted_iota(jnp.int32, sums.shape, 0)
    extra = jnp.where(row == 0, high, jnp.where(row == 1, sums - high, 0.0)).astype(jnp.bfloat16)
    for q in range(send_ref.shape[0]):
        send_ref[q, :TOK, :] = part
        send_ref[q, TOK:, :] = extra
    turned[...] = normed[...].T
    z, c = lax.axis_index("zh"), lax.axis_index("c")
    for mine, out in ((True, own_ref), (False, other_ref)):
        core = c if mine else 1 - c
        first, second = pairings(z, core)
        for x in range(4):
            for place, target in enumerate((z, second, first, lax.bitwise_xor(z, 2))):
                row0 = pl.multiple_of(((x * 4 + target) * 2 + core) * BLOCK, BLOCK)
                at = (x * 4 + place) * BLOCK
                out[at : at + BLOCK, :] = turned[pl.ds(row0, BLOCK), :]


def norm_kernel(parts_ref, g_ref, d_ref, stat_ref, g_scr):
    for place, k in enumerate(CHUNKS):
        g_scr[place * CHUNK : (place + 1) * CHUNK, :] = g_ref[chunk_rows(k), :].astype(jnp.float32)
    n = parts_ref.shape[0]
    one = jnp.zeros((TOK, 1), jnp.float32)
    two = jnp.zeros((TOK, 1), jnp.float32)
    for h in range(d_ref.shape[1] // HEAD_DIM):
        cols = slice(h * HEAD_DIM, (h + 1) * HEAD_DIM)
        raw = sum(parts_ref[q, :TOK, cols].astype(jnp.float32) for q in range(n))
        tail = sum(parts_ref[q, TOK:, cols].astype(jnp.float32) for q in range(n))
        column_sums = jnp.sum(tail, axis=0, keepdims=True)
        g = g_scr[:, cols]
        off = raw - jnp.mean(raw, axis=1, keepdims=True)
        rs = lax.rsqrt(jnp.mean(off * off, axis=1, keepdims=True) + 1e-06)
        z = off * rs
        d = rs * (g - jnp.mean(g, axis=1, keepdims=True) - z * jnp.mean(g * z, axis=1, keepdims=True))
        d = d.astype(jnp.bfloat16)
        d_ref[:, cols] = d
        wide = d.astype(jnp.float32)
        one += jnp.sum(wide * column_sums, axis=1, keepdims=True)
        two += jnp.sum(wide * raw, axis=1, keepdims=True)
    lane = lax.broadcasted_iota(jnp.int32, stat_ref.shape, 1)
    stat_ref[...] = jnp.where(lane == 0, one, two) * (1.0 / D)


def input_grad_kernel(d_ref, w_ref, stat_ref, x_ref, mean_ref, keep_ref, send_ref):
    half = keep_ref.shape[0]
    for out, first in ((send_ref, 4), (keep_ref, 0)):
        at = first * CHUNK
        part = lax.dot_general(
            d_ref[at : at + half, :], w_ref[...], (((1,), (1,)), ((), ())), preferred_element_type=jnp.float32
        )
        for i in range(4):
            rows = chunk_rows(CHUNKS[first + i])
            here = slice(at + i * CHUNK, at + (i + 1) * CHUNK)
            centred = x_ref[rows, :].astype(jnp.float32) - mean_ref[rows, :]
            value = part[i * CHUNK : (i + 1) * CHUNK, :] - stat_ref[here, 0:1] - centred * stat_ref[here, 1:2]
            out[i * CHUNK : (i + 1) * CHUNK, :] = value.astype(jnp.bfloat16)


def weight_grad_kernel(own_ref, other_ref, d_ref, d_other_ref, out_ref):
    rows = out_ref.shape[1]
    for q in range(out_ref.shape[0]):
        at = slice(q * rows, (q + 1) * rows)
        total = jnp.dot(own_ref[at, :], d_ref[...], preferred_element_type=jnp.float32)
        total += jnp.dot(other_ref[at, :], d_other_ref[...], preferred_element_type=jnp.float32)
        out_ref[q] = total.astype(jnp.bfloat16)


def call(kernel, outs, flops, scratch=()):
    return pl.pallas_call(
        kernel,
        out_shape=[jax.ShapeDtypeStruct(s, t) for s, t in outs],
        scratch_shapes=[pltpu.VMEM(s, t) for s, t in scratch],
        compiler_params=pltpu.CompilerParams(vmem_limit_bytes=40 * 1024 * 1024),
        cost_estimate=pl.CostEstimate(flops=flops, bytes_accessed=4 * 1024 * 1024, transcendentals=0),
    )


def per_device(x, mean, weight, grads):
    bf, f32 = jnp.bfloat16, jnp.float32
    tokens, width = x.shape
    cols = 2 * weight.shape[2]
    w = weight.reshape(width, cols)
    g = grads.reshape(tokens, cols)
    mean = mean.reshape(tokens, 1)
    half = width // 2
    work = 2 * tokens * width * cols
    send, own, other = call(
        project_kernel,
        [((4, tokens + EXTRA, cols), bf), ((half, tokens), bf), ((half, tokens), bf)],
        work,
        [((tokens, width), bf), ((width, tokens), bf)],
    )(x, mean, w)
    core_swap = [(0, 1), (1, 0)]
    other = lax.ppermute(other, "c", core_swap)
    parts = lax.all_to_all(send, "mx", 0, 0)
    d_raw, stat = call(
        norm_kernel, [((tokens, cols), bf), ((tokens, 128), f32)], 40 * tokens * cols, [((tokens, cols), f32)]
    )(parts, g)
    d_other = lax.ppermute(d_raw, "c", core_swap)
    keep, away = call(input_grad_kernel, [((tokens // 2, width), bf)] * 2, work)(d_raw, w, stat, x, mean)
    (dw,) = call(weight_grad_kernel, [((4, half // 4, cols), bf)], work)(own, other, d_raw, d_other)

    for bit in (1, 2, 4):
        got = lax.ppermute(away, "my", [(i, i ^ bit) for i in range(8)])
        total = keep.astype(f32) + got.astype(f32)
        n = total.shape[0] // 2
        if bit < 4:
            keep, away = total[:n], total[n:].astype(bf)
    input_grad = total.astype(bf)

    got = lax.all_to_all(dw, "x", 0, 0)
    total = jnp.sum(got.astype(f32), axis=0)
    for step in range(2):
        n = total.shape[0] // 2
        keep, away = total[:n], total[n:].astype(bf)
        pairs = []
        for z in range(4):
            for c in range(2):
                partner = (z ^ 1) if step == c else 3 - z
                pairs.append((2 * z + c, 2 * partner + c))
        got = lax.ppermute(away, ("zh", "c"), pairs)
        total = keep + got.astype(f32)
    return input_grad, total.reshape(BLOCK, 2, cols // 2)


def solution(mesh):
    fine = Mesh(mesh.devices.reshape(4, 4, 2, 4, 8), ("x", "zh", "c", "mx", "my"))
    dp = ("x", "zh", "c")
    return jax.shard_map(
        per_device,
        mesh=fine,
        in_specs=(P(dp, "mx"), P(dp), P("mx", None, "my"), P(dp, None, "my")),
        out_specs=(P((*dp, "my"), "mx"), P(("mx", *dp), None, "my")),
        check_vma=False,
    )
```

```python
import functools

import jax
import jax.numpy as jnp
from jax import lax
from jax.experimental import pallas as pl
from jax.experimental.pallas import tpu as pltpu
from jax.sharding import Mesh, PartitionSpec as P

D = 6144
HEAD_DIM = 128
CHUNKS = (0, 4, 2, 6, 1, 5, 3, 7)
CHUNK = 32
EXTRA = 16
QUARTER = 64
VMEM = 40 * 1024 * 1024
BLOCK = 48


def chunk_rows(k):
    place = lax.axis_index("my")
    return pl.ds(pl.multiple_of(lax.bitwise_xor(place, k) * CHUNK, CHUNK), CHUNK)


def pairings(z, c):
    near, wrap = lax.bitwise_xor(z, 1), 3 - z
    first = jnp.where(c == 0, near, wrap)
    second = jnp.where(c == 0, wrap, near)
    return first, second


def centre(x_ref, mean_ref, normed):
    by_row = [jnp.broadcast_to(mean_ref[i : i + 1, :], (HEAD_DIM, HEAD_DIM)).T[:, :1] for i in range(2)]
    by_row = jnp.concatenate(by_row, axis=0)
    centred = (x_ref[...].astype(jnp.float32) - by_row).astype(jnp.bfloat16)
    normed[...] = centred


def gather_chunks(x_ref, mean_ref, plain, normed):
    centre(x_ref, mean_ref, plain)
    for place, k in enumerate(CHUNKS):
        normed[place * CHUNK : (place + 1) * CHUNK, :] = plain[chunk_rows(k), :]


def project_kernel(x_ref, mean_ref, w_ref, send_ref, extra_ref, normed, plain):
    gather_chunks(x_ref, mean_ref, plain, normed)
    w = w_ref[...]
    part = jnp.dot(normed[...], w, preferred_element_type=jnp.float32).astype(jnp.bfloat16)
    for q in range(send_ref.shape[0]):
        send_ref[q] = part[q * QUARTER : (q + 1) * QUARTER, :]
    ones = jnp.ones((EXTRA, w.shape[0]), jnp.bfloat16)
    sums = jnp.dot(ones, w, preferred_element_type=jnp.float32)
    high = sums.astype(jnp.bfloat16).astype(jnp.float32)
    row = lax.broadcasted_iota(jnp.int32, sums.shape, 0)
    extra = jnp.where(row == 0, high, jnp.where(row == 1, sums - high, 0.0))
    extra_ref[...] = extra.astype(jnp.bfloat16)


def norm_kernel(parts_ref, g_ref, extra_ref, out_ref):
    n = parts_ref.shape[0]
    y = lax.axis_index("mx")
    low = 2 * lax.rem(y, 2) + lax.div(y, 2)
    upper, lower = chunk_rows(low), chunk_rows(low + 4)
    two = jnp.zeros((QUARTER, HEAD_DIM), jnp.float32)
    for h in range(out_ref.shape[2] // HEAD_DIM):
        cols = slice(h * HEAD_DIM, (h + 1) * HEAD_DIM)
        raw = sum(parts_ref[q, :, cols].astype(jnp.float32) for q in range(n))
        g = jnp.concatenate([g_ref[upper, cols], g_ref[lower, cols]], axis=0).astype(jnp.float32)
        off = raw - jnp.mean(raw, axis=1, keepdims=True)
        rs = lax.rsqrt(jnp.mean(off * off, axis=1, keepdims=True) + 1e-06)
        z = off * rs
        d = rs * (g - jnp.mean(g, axis=1, keepdims=True) - z * jnp.mean(g * z, axis=1, keepdims=True))
        d = d.astype(jnp.bfloat16)
        for q in range(n):
            out_ref[q, :QUARTER, cols] = d
        two += d.astype(jnp.float32) * raw
    two = jnp.sum(two, axis=1, keepdims=True)
    high = two.astype(jnp.bfloat16).astype(jnp.float32)
    lane = lax.broadcasted_iota(jnp.int32, (QUARTER, HEAD_DIM), 1)
    stat = jnp.where(lane == 2, high, jnp.where(lane == 3, two - high, 0.0))
    stat = jnp.concatenate([stat, jnp.zeros_like(stat)], axis=0).T[:EXTRA, :].astype(jnp.bfloat16)
    for q in range(n):
        out_ref[q, QUARTER:, :HEAD_DIM] = extra_ref[:, :HEAD_DIM] + stat
        out_ref[q, QUARTER:, HEAD_DIM:] = extra_ref[:, HEAD_DIM:]


def input_grad_kernel(d_ref, w_ref, x_ref, mean_ref, keep_ref, send_ref, d_all, centred_all):
    n = d_ref.shape[0]
    by_row = [jnp.broadcast_to(mean_ref[i : i + 1, :], (HEAD_DIM, HEAD_DIM)).T[:, :1] for i in range(2)]
    centred_all[...] = x_ref[...].astype(jnp.float32) - jnp.concatenate(by_row, axis=0)
    for q in range(n):
        d_all[q * QUARTER : (q + 1) * QUARTER, :] = d_ref[q, :QUARTER, :]
    across = (((1,), (1,)), ((), ()))
    extra = jnp.concatenate([d_ref[q, QUARTER:, :] for q in range(n)], axis=0)
    one = lax.dot_general(d_all[...], extra, across, preferred_element_type=jnp.float32)
    lane = lax.broadcasted_iota(jnp.int32, one.shape, 1)
    one = jnp.sum(jnp.where(lax.rem(lane, EXTRA) < 2, one, 0.0), axis=1, keepdims=True) * (1.0 / D)
    two = [d_ref[q, QUARTER:, :HEAD_DIM].astype(jnp.float32).T[:QUARTER, :] for q in range(n)]
    two = jnp.concatenate([(t[:, 2:3] + t[:, 3:4]) * (1.0 / D) for t in two], axis=0)
    half = keep_ref.shape[0]
    for out, first in ((send_ref, 4), (keep_ref, 0)):
        at = first * CHUNK
        part = lax.dot_general(d_all[at : at + half, :], w_ref[...], across, preferred_element_type=jnp.float32)
        for i in range(4):
            rows = chunk_rows(CHUNKS[first + i])
            here = slice(at + i * CHUNK, at + (i + 1) * CHUNK)
            centred = centred_all[rows, :]
            value = part[i * CHUNK : (i + 1) * CHUNK, :] - one[here, :] - centred * two[here, :]
            out[i * CHUNK : (i + 1) * CHUNK, :] = value.astype(jnp.bfloat16)


def weight_grad_kernel(d_ref, x_ref, mean_ref, mine_ref, away_ref, d_all, normed, plain, total):
    for q in range(d_ref.shape[0]):
        d_all[q * QUARTER : (q + 1) * QUARTER, :] = d_ref[q, :QUARTER, :]
    gather_chunks(x_ref, mean_ref, plain, normed)
    total[...] = jnp.dot(normed[...].T, d_all[...], preferred_element_type=jnp.float32)
    z, c = lax.axis_index("zh"), lax.axis_index("c")
    for core, out in ((1 - c, away_ref), (c, mine_ref)):
        first, second = pairings(z, core)
        for x in range(4):
            for place, target in enumerate((z, second, first, lax.bitwise_xor(z, 2))):
                row0 = pl.multiple_of(((x * 4 + target) * 2 + core) * BLOCK, BLOCK)
                at = (x * 4 + place) * BLOCK
                out[at : at + BLOCK, :] = total[pl.ds(row0, BLOCK), :].astype(out.dtype)


def call(kernel, outs, flops, scratch=()):
    return pl.pallas_call(
        kernel,
        out_shape=[jax.ShapeDtypeStruct(s, t) for s, t in outs],
        scratch_shapes=[pltpu.VMEM(s, t) for s, t in scratch],
        compiler_params=pltpu.CompilerParams(vmem_limit_bytes=VMEM),
        cost_estimate=pl.CostEstimate(flops=flops, bytes_accessed=4 * 1024 * 1024, transcendentals=0),
    )


def per_device(x, mean, weight, grads):
    bf, f32 = jnp.bfloat16, jnp.float32
    tokens, width = x.shape
    cols = 2 * weight.shape[2]
    w = weight.reshape(width, cols)
    g = grads.reshape(tokens, cols)
    mean = mean.reshape(2, tokens // 2)
    half = width // 2
    work = 2 * tokens * width * cols
    whole = (tokens, width), bf
    send, extra = call(project_kernel, [((4, QUARTER, cols), bf), ((EXTRA, cols), bf)], work, [whole, whole])(x, mean, w)
    parts = lax.all_to_all(send, "mx", 0, 0)
    (d_mine,) = call(norm_kernel, [((4, QUARTER + EXTRA, cols), bf)], 10 * tokens * cols)(parts, g, extra)
    d = lax.all_to_all(d_mine, "mx", 0, 0)
    flat = (tokens, cols), bf
    mine, other = call(
        weight_grad_kernel, [((half, cols), bf)] * 2, work, [flat, whole, whole, ((width, cols), f32)]
    )(d, x, mean)
    got = lax.ppermute(other, "c", [(0, 1), (1, 0)])
    keep, away = call(
        input_grad_kernel, [((tokens // 2, width), bf)] * 2, work, [flat, ((tokens, width), f32)]
    )(d, w, x, mean)
    dw = (mine.astype(f32) + got.astype(f32)).astype(bf).reshape(4, half // 4, cols)

    for bit in (1, 2, 4):
        got = lax.ppermute(away, "my", [(i, i ^ bit) for i in range(8)])
        total = keep.astype(f32) + got.astype(f32)
        n = total.shape[0] // 2
        if bit < 4:
            keep, away = total[:n], total[n:].astype(bf)
    input_grad = total.astype(bf)

    got = lax.all_to_all(dw, "x", 0, 0)
    total = jnp.sum(got.astype(f32), axis=0)
    for step in range(2):
        n = total.shape[0] // 2
        keep, away = total[:n], total[n:].astype(bf)
        pairs = []
        for z in range(4):
            for c in range(2):
                partner = (z ^ 1) if step == c else 3 - z
                pairs.append((2 * z + c, 2 * partner + c))
        got = lax.ppermute(away, ("zh", "c"), pairs)
        total = keep + got.astype(f32)
    return input_grad, total.reshape(BLOCK, 2, cols // 2)


def solution(mesh):
    fine = Mesh(mesh.devices.reshape(4, 4, 2, 4, 8), ("x", "zh", "c", "mx", "my"))
    dp = ("x", "zh", "c")
    return jax.shard_map(
        per_device,
        mesh=fine,
        in_specs=(P(dp, "mx"), P(dp), P("mx", None, "my"), P(dp, None, "my")),
        out_specs=(P((*dp, "my"), "mx"), P(("mx", *dp), None, "my")),
        check_vma=False,
    )
```

```python
import functools

import jax
import jax.numpy as jnp
from jax import lax
from jax.experimental import pallas as pl
from jax.experimental.pallas import tpu as pltpu
from jax.sharding import Mesh, PartitionSpec as P

D = 6144
HEAD_DIM = 128
CHUNKS = (0, 4, 2, 6, 1, 5, 3, 7)
CHUNK = 32
EXTRA = 16
QUARTER = 64
VMEM = 40 * 1024 * 1024
BLOCK = 48


def chunk_rows(k):
    place = lax.axis_index("my")
    return pl.ds(pl.multiple_of(lax.bitwise_xor(place, k) * CHUNK, CHUNK), CHUNK)


def pairings(z, c):
    near, wrap = lax.bitwise_xor(z, 1), 3 - z
    first = jnp.where(c == 0, near, wrap)
    second = jnp.where(c == 0, wrap, near)
    return first, second


def centre(x_ref, mean_ref, normed):
    by_row = [jnp.broadcast_to(mean_ref[i : i + 1, :], (HEAD_DIM, HEAD_DIM)).T[:, :1] for i in range(2)]
    by_row = jnp.concatenate(by_row, axis=0)
    centred = (x_ref[...].astype(jnp.float32) - by_row).astype(jnp.bfloat16)
    normed[...] = centred


def gather_chunks(x_ref, mean_ref, plain, normed):
    centre(x_ref, mean_ref, plain)
    for place, k in enumerate(CHUNKS):
        normed[place * CHUNK : (place + 1) * CHUNK, :] = plain[chunk_rows(k), :]


def project_kernel(x_ref, mean_ref, w_ref, send_ref, extra_ref, normed, plain):
    gather_chunks(x_ref, mean_ref, plain, normed)
    w = w_ref[...]
    part = jnp.dot(normed[...], w, preferred_element_type=jnp.float32).astype(jnp.bfloat16)
    for q in range(send_ref.shape[0]):
        send_ref[q] = part[q * QUARTER : (q + 1) * QUARTER, :]
    ones = jnp.ones((EXTRA, w.shape[0]), jnp.bfloat16)
    sums = jnp.dot(ones, w, preferred_element_type=jnp.float32)
    high = sums.astype(jnp.bfloat16).astype(jnp.float32)
    row = lax.broadcasted_iota(jnp.int32, sums.shape, 0)
    extra = jnp.where(row == 0, high, jnp.where(row == 1, sums - high, 0.0))
    extra_ref[...] = extra.astype(jnp.bfloat16)


def norm_kernel(parts_ref, g_ref, extra_ref, out_ref):
    n = parts_ref.shape[0]
    y = lax.axis_index("mx")
    low = 2 * lax.rem(y, 2) + lax.div(y, 2)
    upper, lower = chunk_rows(low), chunk_rows(low + 4)
    two = jnp.zeros((QUARTER, HEAD_DIM), jnp.float32)
    for h in range(out_ref.shape[2] // HEAD_DIM):
        cols = slice(h * HEAD_DIM, (h + 1) * HEAD_DIM)
        raw = sum(parts_ref[q, :, cols].astype(jnp.float32) for q in range(n))
        g = jnp.concatenate([g_ref[upper, cols], g_ref[lower, cols]], axis=0).astype(jnp.float32)
        off = raw - jnp.mean(raw, axis=1, keepdims=True)
        rs = lax.rsqrt(jnp.mean(off * off, axis=1, keepdims=True) + 1e-06)
        z = off * rs
        d = rs * (g - jnp.mean(g, axis=1, keepdims=True) - z * jnp.mean(g * z, axis=1, keepdims=True))
        d = d.astype(jnp.bfloat16)
        for q in range(n):
            out_ref[q, :QUARTER, cols] = d
        two += d.astype(jnp.float32) * raw
    two = jnp.sum(two, axis=1, keepdims=True)
    high = two.astype(jnp.bfloat16).astype(jnp.float32)
    lane = lax.broadcasted_iota(jnp.int32, (QUARTER, HEAD_DIM), 1)
    stat = jnp.where(lane == 2, high, jnp.where(lane == 3, two - high, 0.0))
    stat = jnp.concatenate([stat, jnp.zeros_like(stat)], axis=0).T[:EXTRA, :].astype(jnp.bfloat16)
    for q in range(n):
        out_ref[q, QUARTER:, :HEAD_DIM] = extra_ref[:, :HEAD_DIM] + stat
        out_ref[q, QUARTER:, HEAD_DIM:] = extra_ref[:, HEAD_DIM:]


def input_grad_kernel(d_ref, w_ref, x_ref, mean_ref, keep_ref, send_ref, d_all, centred_all):
    n = d_ref.shape[0]
    by_row = [jnp.broadcast_to(mean_ref[i : i + 1, :], (HEAD_DIM, HEAD_DIM)).T[:, :1] for i in range(2)]
    centred_all[...] = x_ref[...].astype(jnp.float32) - jnp.concatenate(by_row, axis=0)
    for q in range(n):
        d_all[q * QUARTER : (q + 1) * QUARTER, :] = d_ref[q, :QUARTER, :]
    across = (((1,), (1,)), ((), ()))
    extra = jnp.concatenate([d_ref[q, QUARTER:, :] for q in range(n)], axis=0)
    one = lax.dot_general(d_all[...], extra, across, preferred_element_type=jnp.float32)
    lane = lax.broadcasted_iota(jnp.int32, one.shape, 1)
    one = jnp.sum(jnp.where(lax.rem(lane, EXTRA) < 2, one, 0.0), axis=1, keepdims=True) * (1.0 / D)
    two = [d_ref[q, QUARTER:, :HEAD_DIM].astype(jnp.float32).T[:QUARTER, :] for q in range(n)]
    two = jnp.concatenate([(t[:, 2:3] + t[:, 3:4]) * (1.0 / D) for t in two], axis=0)
    half = keep_ref.shape[0]
    for out, first in ((send_ref, 4), (keep_ref, 0)):
        at = first * CHUNK
        part = lax.dot_general(d_all[at : at + half, :], w_ref[...], across, preferred_element_type=jnp.float32)
        for i in range(4):
            rows = chunk_rows(CHUNKS[first + i])
            here = slice(at + i * CHUNK, at + (i + 1) * CHUNK)
            centred = centred_all[rows, :]
            value = part[i * CHUNK : (i + 1) * CHUNK, :] - one[here, :] - centred * two[here, :]
            out[i * CHUNK : (i + 1) * CHUNK, :] = value.astype(jnp.bfloat16)


def weight_grad_kernel(d_ref, x_ref, mean_ref, mine_ref, away_ref, d_all, normed, plain, total):
    for q in range(d_ref.shape[0]):
        d_all[q * QUARTER : (q + 1) * QUARTER, :] = d_ref[q, :QUARTER, :]
    gather_chunks(x_ref, mean_ref, plain, normed)
    total[...] = jnp.dot(normed[...].T, d_all[...], preferred_element_type=jnp.float32)
    z, c = lax.axis_index("zh"), lax.axis_index("c")
    for core, out in ((1 - c, away_ref), (c, mine_ref)):
        first, second = pairings(z, core)
        order = [(x, lax.bitwise_xor(z, 2)) for x in range(4)]
        order += [(x, target) for x in range(4) for target in (z, second, first)]
        for place, (x, target) in enumerate(order):
            row0 = pl.multiple_of(((x * 4 + target) * 2 + core) * BLOCK, BLOCK)
            out[place * BLOCK : (place + 1) * BLOCK, :] = total[pl.ds(row0, BLOCK), :].astype(out.dtype)


def call(kernel, outs, flops, scratch=()):
    return pl.pallas_call(
        kernel,
        out_shape=[jax.ShapeDtypeStruct(s, t) for s, t in outs],
        scratch_shapes=[pltpu.VMEM(s, t) for s, t in scratch],
        compiler_params=pltpu.CompilerParams(vmem_limit_bytes=VMEM),
        cost_estimate=pl.CostEstimate(flops=flops, bytes_accessed=4 * 1024 * 1024, transcendentals=0),
    )


def per_device(x, mean, weight, grads):
    bf, f32 = jnp.bfloat16, jnp.float32
    tokens, width = x.shape
    cols = 2 * weight.shape[2]
    w = weight.reshape(width, cols)
    g = grads.reshape(tokens, cols)
    mean = mean.reshape(2, tokens // 2)
    half = width // 2
    work = 2 * tokens * width * cols
    whole = (tokens, width), bf
    send, extra = call(project_kernel, [((4, QUARTER, cols), bf), ((EXTRA, cols), bf)], work, [whole, whole])(x, mean, w)
    parts = lax.all_to_all(send, "mx", 0, 0)
    (d_mine,) = call(norm_kernel, [((4, QUARTER + EXTRA, cols), bf)], 10 * tokens * cols)(parts, g, extra)
    d = lax.all_to_all(d_mine, "mx", 0, 0)
    flat = (tokens, cols), bf
    mine, other = call(
        weight_grad_kernel, [((half, cols), bf)] * 2, work, [flat, whole, whole, ((width, cols), f32)]
    )(d, x, mean)
    got = lax.ppermute(other, "c", [(0, 1), (1, 0)])
    keep, away = call(
        input_grad_kernel, [((tokens // 2, width), bf)] * 2, work, [flat, ((tokens, width), f32)]
    )(d, w, x, mean)
    dw = (mine.astype(f32) + got.astype(f32)).astype(bf)
    relay, rest = dw[: 4 * BLOCK].reshape(4, BLOCK, cols), dw[4 * BLOCK :].reshape(4, 3 * BLOCK, cols)

    for bit in (1, 2, 4):
        got = lax.ppermute(away, "my", [(i, i ^ bit) for i in range(8)])
        total = keep.astype(f32) + got.astype(f32)
        n = total.shape[0] // 2
        if bit < 4:
            keep, away = total[:n], total[n:].astype(bf)
    input_grad = total.astype(bf)

    def swap_zh(chunk, step):
        pairs = []
        for z in range(4):
            for c in range(2):
                partner = (z ^ 1) if step == c else 3 - z
                pairs.append((2 * z + c, 2 * partner + c))
        return lax.ppermute(chunk, ("zh", "c"), pairs).astype(f32)

    def over_x(parts):
        return jnp.sum(lax.all_to_all(parts, "x", 0, 0).astype(f32), axis=0)

    relayed = swap_zh(over_x(relay).astype(bf), 0)
    rest = over_x(rest)
    own, passed, straight = rest[:BLOCK], rest[BLOCK : 2 * BLOCK], rest[2 * BLOCK :]
    own = own + swap_zh(straight.astype(bf), 0)
    total = own + swap_zh((passed + relayed).astype(bf), 1)
    return input_grad, total.reshape(BLOCK, 2, cols // 2)


def solution(mesh):
    fine = Mesh(mesh.devices.reshape(4, 4, 2, 4, 8), ("x", "zh", "c", "mx", "my"))
    dp = ("x", "zh", "c")
    return jax.shard_map(
        per_device,
        mesh=fine,
        in_specs=(P(dp, "mx"), P(dp), P("mx", None, "my"), P(dp, None, "my")),
        out_specs=(P((*dp, "my"), "mx"), P(("mx", *dp), None, "my")),
        check_vma=False,
    )
```

```python
import functools

import jax
import jax.numpy as jnp
from jax import lax
from jax.experimental import pallas as pl
from jax.experimental.pallas import tpu as pltpu
from jax.sharding import Mesh, PartitionSpec as P

D = 6144
HEAD_DIM = 128
CHUNKS = (0, 4, 2, 6, 1, 5, 3, 7)
CHUNK = 32
EXTRA = 16
QUARTER = 64
VMEM = 40 * 1024 * 1024
BLOCK = 48


def chunk_rows(k):
    place = lax.axis_index("my")
    return pl.ds(pl.multiple_of(lax.bitwise_xor(place, k) * CHUNK, CHUNK), CHUNK)


def pairings(z, c):
    near, wrap = lax.bitwise_xor(z, 1), 3 - z
    first = jnp.where(c == 0, near, wrap)
    second = jnp.where(c == 0, wrap, near)
    return first, second


def centre(x_ref, mean_ref, normed):
    by_row = [jnp.broadcast_to(mean_ref[i : i + 1, :], (HEAD_DIM, HEAD_DIM)).T[:, :1] for i in range(2)]
    by_row = jnp.concatenate(by_row, axis=0)
    centred = (x_ref[...].astype(jnp.float32) - by_row).astype(jnp.bfloat16)
    normed[...] = centred


def gather_chunks(x_ref, mean_ref, plain, normed):
    centre(x_ref, mean_ref, plain)
    for place, k in enumerate(CHUNKS):
        normed[place * CHUNK : (place + 1) * CHUNK, :] = plain[chunk_rows(k), :]


def project_kernel(x_ref, mean_ref, w_ref, send_ref, extra_ref, normed, plain):
    gather_chunks(x_ref, mean_ref, plain, normed)
    w = w_ref[...]
    part = jnp.dot(normed[...], w, preferred_element_type=jnp.float32).astype(jnp.bfloat16)
    for q in range(send_ref.shape[0]):
        send_ref[q] = part[q * QUARTER : (q + 1) * QUARTER, :]
    ones = jnp.ones((EXTRA, w.shape[0]), jnp.bfloat16)
    sums = jnp.dot(ones, w, preferred_element_type=jnp.float32)
    high = sums.astype(jnp.bfloat16).astype(jnp.float32)
    row = lax.broadcasted_iota(jnp.int32, sums.shape, 0)
    extra = jnp.where(row == 0, high, jnp.where(row == 1, sums - high, 0.0))
    extra_ref[...] = extra.astype(jnp.bfloat16)


def norm_kernel(parts_ref, g_ref, extra_ref, out_ref):
    n = parts_ref.shape[0]
    y = lax.axis_index("mx")
    low = 2 * lax.rem(y, 2) + lax.div(y, 2)
    upper, lower = chunk_rows(low), chunk_rows(low + 4)
    two = jnp.zeros((QUARTER, HEAD_DIM), jnp.float32)
    for h in range(out_ref.shape[2] // HEAD_DIM):
        cols = slice(h * HEAD_DIM, (h + 1) * HEAD_DIM)
        raw = sum(parts_ref[q, :, cols].astype(jnp.float32) for q in range(n))
        g = jnp.concatenate([g_ref[upper, cols], g_ref[lower, cols]], axis=0).astype(jnp.float32)
        off = raw - jnp.mean(raw, axis=1, keepdims=True)
        rs = lax.rsqrt(jnp.mean(off * off, axis=1, keepdims=True) + 1e-06)
        z = off * rs
        d = rs * (g - jnp.mean(g, axis=1, keepdims=True) - z * jnp.mean(g * z, axis=1, keepdims=True))
        d = d.astype(jnp.bfloat16)
        for q in range(n):
            out_ref[q, :QUARTER, cols] = d
        two += d.astype(jnp.float32) * raw
    two = jnp.sum(two, axis=1, keepdims=True)
    high = two.astype(jnp.bfloat16).astype(jnp.float32)
    lane = lax.broadcasted_iota(jnp.int32, (QUARTER, HEAD_DIM), 1)
    stat = jnp.where(lane == 2, high, jnp.where(lane == 3, two - high, 0.0))
    stat = jnp.concatenate([stat, jnp.zeros_like(stat)], axis=0).T[:EXTRA, :].astype(jnp.bfloat16)
    for q in range(n):
        out_ref[q, QUARTER:, :HEAD_DIM] = extra_ref[:, :HEAD_DIM] + stat
        out_ref[q, QUARTER:, HEAD_DIM:] = extra_ref[:, HEAD_DIM:]


def input_grad_kernel(d_ref, w_ref, x_ref, mean_ref, keep_ref, send_ref, d_all, centred_all):
    n = d_ref.shape[0]
    by_row = [jnp.broadcast_to(mean_ref[i : i + 1, :], (HEAD_DIM, HEAD_DIM)).T[:, :1] for i in range(2)]
    centred_all[...] = x_ref[...].astype(jnp.float32) - jnp.concatenate(by_row, axis=0)
    for q in range(n):
        d_all[q * QUARTER : (q + 1) * QUARTER, :] = d_ref[q, :QUARTER, :]
    across = (((1,), (1,)), ((), ()))
    extra = jnp.concatenate([d_ref[q, QUARTER:, :] for q in range(n)], axis=0)
    one = lax.dot_general(d_all[...], extra, across, preferred_element_type=jnp.float32)
    lane = lax.broadcasted_iota(jnp.int32, one.shape, 1)
    one = jnp.sum(jnp.where(lax.rem(lane, EXTRA) < 2, one, 0.0), axis=1, keepdims=True) * (1.0 / D)
    two = [d_ref[q, QUARTER:, :HEAD_DIM].astype(jnp.float32).T[:QUARTER, :] for q in range(n)]
    two = jnp.concatenate([(t[:, 2:3] + t[:, 3:4]) * (1.0 / D) for t in two], axis=0)
    half = keep_ref.shape[0]
    for out, first in ((send_ref, 4), (keep_ref, 0)):
        at = first * CHUNK
        part = lax.dot_general(d_all[at : at + half, :], w_ref[...], across, preferred_element_type=jnp.float32)
        for i in range(4):
            rows = chunk_rows(CHUNKS[first + i])
            here = slice(at + i * CHUNK, at + (i + 1) * CHUNK)
            centred = centred_all[rows, :]
            value = part[i * CHUNK : (i + 1) * CHUNK, :] - one[here, :] - centred * two[here, :]
            out[i * CHUNK : (i + 1) * CHUNK, :] = value.astype(jnp.bfloat16)


def weight_grad_kernel(d_ref, x_ref, mean_ref, mine_ref, away_ref, d_all, normed, plain, total):
    for q in range(d_ref.shape[0]):
        d_all[q * QUARTER : (q + 1) * QUARTER, :] = d_ref[q, :QUARTER, :]
    gather_chunks(x_ref, mean_ref, plain, normed)
    total[...] = jnp.dot(normed[...].T, d_all[...], preferred_element_type=jnp.float32)
    z, c = lax.axis_index("zh"), lax.axis_index("c")
    for core, out in ((1 - c, away_ref), (c, mine_ref)):
        first, second = pairings(z, core)
        for x in range(4):
            for place, target in enumerate((z, second, first, lax.bitwise_xor(z, 2))):
                row0 = pl.multiple_of(((x * 4 + target) * 2 + core) * BLOCK, BLOCK)
                at = (x * 4 + place) * BLOCK
                out[at : at + BLOCK, :] = total[pl.ds(row0, BLOCK), :].astype(out.dtype)


def call(kernel, outs, flops, scratch=()):
    return pl.pallas_call(
        kernel,
        out_shape=[jax.ShapeDtypeStruct(s, t) for s, t in outs],
        scratch_shapes=[pltpu.VMEM(s, t) for s, t in scratch],
        compiler_params=pltpu.CompilerParams(vmem_limit_bytes=VMEM),
        cost_estimate=pl.CostEstimate(flops=flops, bytes_accessed=4 * 1024 * 1024, transcendentals=0),
    )


def per_device(x, mean, weight, grads):
    bf, f32 = jnp.bfloat16, jnp.float32
    tokens, width = x.shape
    cols = 2 * weight.shape[2]
    w = weight.reshape(width, cols)
    g = grads.reshape(tokens, cols)
    mean = mean.reshape(2, tokens // 2)
    half = width // 2
    work = 2 * tokens * width * cols
    whole = (tokens, width), bf
    send, extra = call(project_kernel, [((4, QUARTER, cols), bf), ((EXTRA, cols), bf)], work, [whole, whole])(x, mean, w)
    parts = lax.all_to_all(send, "mx", 0, 0)
    (d_mine,) = call(norm_kernel, [((4, QUARTER + EXTRA, cols), bf)], 10 * tokens * cols)(parts, g, extra)
    d = lax.all_to_all(d_mine, "mx", 0, 0)
    flat = (tokens, cols), bf
    mine, other = call(
        weight_grad_kernel, [((half, cols), bf)] * 2, work, [flat, whole, whole, ((width, cols), f32)]
    )(d, x, mean)
    got = lax.ppermute(other, "c", [(0, 1), (1, 0)])
    keep, away = call(
        input_grad_kernel, [((tokens // 2, width), bf)] * 2, work, [flat, ((tokens, width), f32)]
    )(d, w, x, mean)
    dw = (mine.astype(f32) + got.astype(f32)).astype(bf).reshape(4, half // 4, cols)

    def swap_zh(chunk, step):
        pairs = []
        for z in range(4):
            for c in range(2):
                partner = (z ^ 1) if step == c else 3 - z
                pairs.append((2 * z + c, 2 * partner + c))
        return lax.ppermute(chunk.astype(bf), ("zh", "c"), pairs).astype(f32)

    def swap_my(away, bit):
        return lax.ppermute(away, "my", [(i, i ^ bit) for i in range(8)])

    got = swap_my(away, 1)
    total = jnp.sum(lax.all_to_all(dw, "x", 0, 0).astype(f32), axis=0)
    got, total = lax.optimization_barrier((got, total))
    own, passed, straight, relay = [total[i * BLOCK : (i + 1) * BLOCK] for i in range(4)]
    relayed = swap_zh(relay, 0)
    total = keep.astype(f32) + got.astype(f32)
    n = total.shape[0] // 2
    total = total[:n] + swap_my(total[n:].astype(bf), 2).astype(f32)
    n //= 2
    keep, away = total[:n], total[n:].astype(bf)
    input_grad = (keep + swap_my(away, 4).astype(f32)).astype(bf)
    own = own + swap_zh(straight, 0)
    total = own + swap_zh(passed + relayed, 1)
    return input_grad, total.reshape(BLOCK, 2, cols // 2)


def solution(mesh):
    fine = Mesh(mesh.devices.reshape(4, 4, 2, 4, 8), ("x", "zh", "c", "mx", "my"))
    dp = ("x", "zh", "c")
    return jax.shard_map(
        per_device,
        mesh=fine,
        in_specs=(P(dp, "mx"), P(dp), P("mx", None, "my"), P(dp, None, "my")),
        out_specs=(P((*dp, "my"), "mx"), P(("mx", *dp), None, "my")),
        check_vma=False,
    )
```

```python
import functools

import jax
import jax.numpy as jnp
from jax import lax
from jax.experimental import pallas as pl
from jax.experimental.pallas import tpu as pltpu
from jax.sharding import Mesh, PartitionSpec as P

D = 6144
HEAD_DIM = 128
CHUNKS = (0, 4, 2, 6, 1, 5, 3, 7)
CHUNK = 32
EXTRA = 16
QUARTER = 64
VMEM = 40 * 1024 * 1024
BLOCK = 48


def chunk_rows(k):
    place = lax.axis_index("my")
    return pl.ds(pl.multiple_of(lax.bitwise_xor(place, k) * CHUNK, CHUNK), CHUNK)


def pairings(z, c):
    near, wrap = lax.bitwise_xor(z, 1), 3 - z
    first = jnp.where(c == 0, near, wrap)
    second = jnp.where(c == 0, wrap, near)
    return first, second


def centre(x_ref, mean_ref, normed):
    by_row = [jnp.broadcast_to(mean_ref[i : i + 1, :], (HEAD_DIM, HEAD_DIM)).T[:, :1] for i in range(2)]
    by_row = jnp.concatenate(by_row, axis=0)
    centred = (x_ref[...].astype(jnp.float32) - by_row).astype(jnp.bfloat16)
    normed[...] = centred


def gather_chunks(x_ref, mean_ref, plain, normed):
    centre(x_ref, mean_ref, plain)
    for place, k in enumerate(CHUNKS):
        normed[place * CHUNK : (place + 1) * CHUNK, :] = plain[chunk_rows(k), :]


def project_kernel(x_ref, mean_ref, w_ref, send_ref, extra_ref, normed, plain):
    gather_chunks(x_ref, mean_ref, plain, normed)
    w = w_ref[...]
    part = jnp.dot(normed[...], w, preferred_element_type=jnp.float32).astype(jnp.bfloat16)
    for q in range(send_ref.shape[0]):
        send_ref[q] = part[q * QUARTER : (q + 1) * QUARTER, :]
    ones = jnp.ones((EXTRA, w.shape[0]), jnp.bfloat16)
    sums = jnp.dot(ones, w, preferred_element_type=jnp.float32)
    high = sums.astype(jnp.bfloat16).astype(jnp.float32)
    row = lax.broadcasted_iota(jnp.int32, sums.shape, 0)
    extra = jnp.where(row == 0, high, jnp.where(row == 1, sums - high, 0.0))
    extra_ref[...] = extra.astype(jnp.bfloat16)


def norm_kernel(parts_ref, g_ref, extra_ref, out_ref):
    n = parts_ref.shape[0]
    y = lax.axis_index("mx")
    low = 2 * lax.rem(y, 2) + lax.div(y, 2)
    upper, lower = chunk_rows(low), chunk_rows(low + 4)
    two = jnp.zeros((QUARTER, HEAD_DIM), jnp.float32)
    for h in range(out_ref.shape[2] // HEAD_DIM):
        cols = slice(h * HEAD_DIM, (h + 1) * HEAD_DIM)
        raw = sum(parts_ref[q, :, cols].astype(jnp.float32) for q in range(n))
        g = jnp.concatenate([g_ref[upper, cols], g_ref[lower, cols]], axis=0).astype(jnp.float32)
        off = raw - jnp.mean(raw, axis=1, keepdims=True)
        rs = lax.rsqrt(jnp.mean(off * off, axis=1, keepdims=True) + 1e-06)
        z = off * rs
        d = rs * (g - jnp.mean(g, axis=1, keepdims=True) - z * jnp.mean(g * z, axis=1, keepdims=True))
        d = d.astype(jnp.bfloat16)
        for q in range(n):
            out_ref[q, :QUARTER, cols] = d
        two += d.astype(jnp.float32) * raw
    two = jnp.sum(two, axis=1, keepdims=True)
    high = two.astype(jnp.bfloat16).astype(jnp.float32)
    lane = lax.broadcasted_iota(jnp.int32, (QUARTER, HEAD_DIM), 1)
    stat = jnp.where(lane == 2, high, jnp.where(lane == 3, two - high, 0.0))
    stat = jnp.concatenate([stat, jnp.zeros_like(stat)], axis=0).T[:EXTRA, :].astype(jnp.bfloat16)
    for q in range(n):
        out_ref[q, QUARTER:, :HEAD_DIM] = extra_ref[:, :HEAD_DIM] + stat
        out_ref[q, QUARTER:, HEAD_DIM:] = extra_ref[:, HEAD_DIM:]


def input_grad_kernel(d_ref, w_ref, x_ref, mean_ref, keep_ref, send_ref, d_all, centred_all):
    n = d_ref.shape[0]
    by_row = [jnp.broadcast_to(mean_ref[i : i + 1, :], (HEAD_DIM, HEAD_DIM)).T[:, :1] for i in range(2)]
    centred_all[...] = x_ref[...].astype(jnp.float32) - jnp.concatenate(by_row, axis=0)
    for q in range(n):
        d_all[q * QUARTER : (q + 1) * QUARTER, :] = d_ref[q, :QUARTER, :]
    across = (((1,), (1,)), ((), ()))
    extra = jnp.concatenate([d_ref[q, QUARTER:, :] for q in range(n)], axis=0)
    one = lax.dot_general(d_all[...], extra, across, preferred_element_type=jnp.float32)
    lane = lax.broadcasted_iota(jnp.int32, one.shape, 1)
    one = jnp.sum(jnp.where(lax.rem(lane, EXTRA) < 2, one, 0.0), axis=1, keepdims=True) * (1.0 / D)
    two = [d_ref[q, QUARTER:, :HEAD_DIM].astype(jnp.float32).T[:QUARTER, :] for q in range(n)]
    two = jnp.concatenate([(t[:, 2:3] + t[:, 3:4]) * (1.0 / D) for t in two], axis=0)
    half = keep_ref.shape[0]
    for out, first in ((send_ref, 4), (keep_ref, 0)):
        at = first * CHUNK
        part = lax.dot_general(d_all[at : at + half, :], w_ref[...], across, preferred_element_type=jnp.float32)
        for i in range(4):
            rows = chunk_rows(CHUNKS[first + i])
            here = slice(at + i * CHUNK, at + (i + 1) * CHUNK)
            centred = centred_all[rows, :]
            value = part[i * CHUNK : (i + 1) * CHUNK, :] - one[here, :] - centred * two[here, :]
            out[i * CHUNK : (i + 1) * CHUNK, :] = value.astype(jnp.bfloat16)


def weight_grad_kernel(d_ref, x_ref, mean_ref, mine_ref, away_ref, d_all, normed, plain, total):
    for q in range(d_ref.shape[0]):
        d_all[q * QUARTER : (q + 1) * QUARTER, :] = d_ref[q, :QUARTER, :]
    gather_chunks(x_ref, mean_ref, plain, normed)
    total[...] = jnp.dot(normed[...].T, d_all[...], preferred_element_type=jnp.float32)
    z, c = lax.axis_index("zh"), lax.axis_index("c")
    for core, out in ((1 - c, away_ref), (c, mine_ref)):
        first, second = pairings(z, core)
        for x in range(4):
            for place, target in enumerate((z, second, first, lax.bitwise_xor(z, 2))):
                row0 = pl.multiple_of(((x * 4 + target) * 2 + core) * BLOCK, BLOCK)
                at = (x * 4 + place) * BLOCK
                out[at : at + BLOCK, :] = total[pl.ds(row0, BLOCK), :].astype(out.dtype)


def call(kernel, outs, flops, scratch=()):
    return pl.pallas_call(
        kernel,
        out_shape=[jax.ShapeDtypeStruct(s, t) for s, t in outs],
        scratch_shapes=[pltpu.VMEM(s, t) for s, t in scratch],
        compiler_params=pltpu.CompilerParams(vmem_limit_bytes=VMEM),
        cost_estimate=pl.CostEstimate(flops=flops, bytes_accessed=4 * 1024 * 1024, transcendentals=0),
    )


def per_device(x, mean, weight, grads):
    bf, f32 = jnp.bfloat16, jnp.float32
    tokens, width = x.shape
    cols = 2 * weight.shape[2]
    w = weight.reshape(width, cols)
    g = grads.reshape(tokens, cols)
    mean = mean.reshape(2, tokens // 2)
    half = width // 2
    work = 2 * tokens * width * cols
    whole = (tokens, width), bf
    send, extra = call(project_kernel, [((4, QUARTER, cols), bf), ((EXTRA, cols), bf)], work, [whole, whole])(x, mean, w)
    parts = lax.all_to_all(send, "mx", 0, 0)
    (d_mine,) = call(norm_kernel, [((4, QUARTER + EXTRA, cols), bf)], 10 * tokens * cols)(parts, g, extra)
    d = lax.all_to_all(d_mine, "mx", 0, 0)
    flat = (tokens, cols), bf
    mine, other = call(
        weight_grad_kernel, [((half, cols), bf)] * 2, work, [flat, whole, whole, ((width, cols), f32)]
    )(d, x, mean)
    got = lax.ppermute(other, "c", [(0, 1), (1, 0)])
    keep, away = call(
        input_grad_kernel, [((tokens // 2, width), bf)] * 2, work, [flat, ((tokens, width), f32)]
    )(d, w, x, mean)
    dw = (mine.astype(f32) + got.astype(f32)).astype(bf).reshape(4, half // 4, cols)

    for bit in (1, 2, 4):
        got = lax.ppermute(away, "my", [(i, i ^ bit) for i in range(8)])
        total = keep.astype(f32) + got.astype(f32)
        n = total.shape[0] // 2
        if bit < 4:
            keep, away = total[:n], total[n:].astype(bf)
    input_grad = total.astype(bf)

    def swap_zh(chunk, step):
        pairs = []
        for z in range(4):
            for c in range(2):
                partner = (z ^ 1) if step == c else 3 - z
                pairs.append((2 * z + c, 2 * partner + c))
        return lax.ppermute(chunk.astype(bf), ("zh", "c"), pairs).astype(f32)

    total = jnp.sum(lax.all_to_all(dw, "x", 0, 0).astype(f32), axis=0)
    own, passed, straight, relay = [total[i * BLOCK : (i + 1) * BLOCK] for i in range(4)]
    relayed = swap_zh(relay, 0)
    own = own + swap_zh(straight, 0)
    total = own + swap_zh(passed + relayed, 1)
    return input_grad, total.reshape(BLOCK, 2, cols // 2)


def solution(mesh):
    fine = Mesh(mesh.devices.reshape(4, 4, 2, 4, 8), ("x", "zh", "c", "mx", "my"))
    dp = ("x", "zh", "c")
    return jax.shard_map(
        per_device,
        mesh=fine,
        in_specs=(P(dp, "mx"), P(dp), P("mx", None, "my"), P(dp, None, "my")),
        out_specs=(P((*dp, "my"), "mx"), P(("mx", *dp), None, "my")),
        check_vma=False,
    )
```
